128 devices in a mesh: ctx: 32 (over z, x, y_lo), tp: 4 (over y_hi, core).
Axes of the slice: x: 4, y: 4 (y_hi: 2, y_lo: 2; y = y_hi * 2 + y_lo), z: 4, core: 2. Of those that a mesh axis runs over, the one named last changes fastest.
Arguments:
- span_input: bfloat16 [256, 4096], P(None, 'ctx'), may hold values from -24 to 24
- norm_gain: bfloat16 [4096], P('ctx'), may hold values from 0.099609375 to 1.8984375
- query_key_value_weight: bfloat16 [4096, 3, 4096], P('ctx', None, 'tp'), may hold values from -0.1875 to 0.1875
- cache_keys: bfloat16 [131072, 4096], P('ctx', 'tp'), may hold values from -140 to 140
- cache_values: bfloat16 [131072, 4096], P('ctx', 'tp'), may hold values from -6 to 6
- attn_out_weight: bfloat16 [4096, 4096], P('tp', 'ctx'), may hold values from -0.09375 to 0.09375
- mixer_gain: bfloat16 [4096], P('ctx'), may hold values from 0.099609375 to 1.8984375
- hyena_in_weight: bfloat16 [4096, 3, 4096], P('ctx', None, 'tp'), may hold values from -0.09375 to 0.09375
- short_filter: float32 [3, 3, 4096], P(None, None, 'tp'), may hold values from -4 to 4
- short_history: float32 [2, 3, 4096], P(None, None, 'tp'), may hold values from -6 to 6
- conv_history: float32 [127, 4096], P(None, 'tp'), may hold values from -6 to 6
- long_filter: float32 [128, 4096], P(None, 'tp'), may hold values from -2 to 2
- hyena_out_weight: bfloat16 [4096, 4096], P('tp', 'ctx'), may hold values from -0.09375 to 0.09375
Outputs:
- mixed: bfloat16 [256, 4096], P(None, 'ctx')
The draws below stay inside these ranges and needn't reach their ends.
All inputs are finite; a program needn't handle non-finite values.
Results may differ from the reference program's by a relative error of at most 0.014.
The reference program's roundings to bfloat16 on the way count: a program that leaves them out, or rounds other values in their place, can miss the bound.
Values may be sent and summed in bfloat16 or wider, within the bound.
No kernel may reach another device: no remote copies, remote signals or barrier semaphores. Data moves between devices by JAX's collectives and lax.ppermute only.
A program may use at most 192 MiB of HBM per device.

```python
import math
import jax
import jax.numpy as jnp
from jax import lax

D = 4096
HEADS = 32
HDIM = 128
SPAN = 256
TOK_DEV = 8
CACHE_DEV = 4096
CONTEXT = 131072
FILT = 128
HISTORY = 127
SHORT = 3
N_CTX = 32


def draw_span_input(key, part):
    key = jax.random.fold_in(key, 11)
    row_key, base_key = jax.random.split(key, 2)
    row_scales = jnp.exp(jax.random.uniform(row_key, (SPAN, 1), jnp.float32, math.log(0.3), math.log(3.0)))
    column_scales = jnp.exp(math.log(3.0) * jnp.arange(D, dtype=jnp.float32) / D)[None, :]
    base = jnp.clip(jax.random.normal(base_key, (SPAN, D), jnp.float32), -5.0, 5.0)
    return (0.5 * base * row_scales * column_scales).astype(jnp.bfloat16)


def draw_cache_keys(key, part):
    key = jax.random.fold_in(key, 23)
    head_key, rough_key, base_key = jax.random.split(key, 3)
    head_size = D // HEADS
    head_scales = jnp.exp(jax.random.uniform(head_key, (HEADS,), jnp.float32, math.log(1.0), math.log(1.75)))
    column_scale = jnp.repeat(head_scales, head_size)[None, :]
    rough = jnp.exp(jax.random.uniform(rough_key, (CONTEXT, 1), jnp.float32, math.log(0.8), math.log(1.25)))
    base = jnp.clip(jax.random.normal(base_key, (CONTEXT, D), jnp.float32), -6.0, 6.0)
    result = base * column_scale * rough
    return result.astype(jnp.bfloat16)


def draw_long_filter(key, part):
    key = jax.random.fold_in(key, 37)
    rate_key, filter_tap_key = jax.random.split(key, 2)
    rates = jnp.exp(jax.random.uniform(rate_key, (1, D), jnp.float32, math.log(1.0 / 400.0), math.log(1.0 / 20.0)))
    lags = jnp.arange(FILT, dtype=jnp.float32)[:, None]
    taps = jnp.clip(jax.random.normal(filter_tap_key, (FILT, D), jnp.float32), -5.0, 5.0)
    return jnp.clip(taps * jnp.exp(-rates * lags) * (3.0 / math.sqrt(FILT)), -2.0, 2.0)


def shard_levels(own_key, extent, pieces, least, top_value):
    def one(position, blocks):
        heights = jax.random.uniform(jax.random.fold_in(jax.random.fold_in(own_key, 6), position), (blocks,), jnp.float32, least / len(pieces), top_value / len(pieces))
        return jnp.repeat(jnp.exp(heights), extent[position] // blocks).reshape((-1,) + (1,) * (len(extent) - position - 1))

    level = one(*pieces[0])
    for cut in pieces[1:]:
        level = level * one(*cut)
    return level


def scatter_about(rng, dims, width, limit, cuts=(), kind=jnp.bfloat16):
    drawn = width * jax.random.normal(rng, dims, jnp.float32)
    if cuts:
        drawn = drawn * shard_levels(rng, dims, cuts, -0.22, 0.18)
    return jnp.clip(drawn, -limit, limit).astype(kind)


def setup_inputs(seed: int = 0) -> dict:
    keys = jax.random.split(jax.random.key(seed), 14)
    span_input = draw_span_input(jax.random.fold_in(keys[13], 71), 0)
    norm_gain = jnp.clip(1.0 + 0.18 * jax.random.normal(keys[1], (D,), jnp.float32), 0.099609375, 1.8984375).astype(jnp.bfloat16)
    query_key_value_weight = scatter_about(keys[2], (D, 3, D), (D // 4) ** -0.5, 0.1875, ((0, 32), (2, 4)))
    cache_keys = draw_cache_keys(jax.random.fold_in(keys[13], 71), 0)
    cache_values = scatter_about(keys[4], (CONTEXT, D), 1.0, 6.0, ((0, 32), (1, 4)))
    attn_out_weight = scatter_about(keys[5], (D, D), D ** -0.5, 0.09375, ((0, 4), (1, 32)))
    mixer_gain = jnp.clip(1.0 + 0.18 * jax.random.normal(keys[6], (D,), jnp.float32), 0.099609375, 1.8984375).astype(jnp.bfloat16)
    hyena_in_weight = scatter_about(keys[7], (D, 3, D), D ** -0.5, 0.09375, ((0, 32), (2, 4)))
    short_filter = scatter_about(keys[8], (SHORT, 3, D), 0.6, 4.0, ((2, 4),), jnp.float32)
    short_history = scatter_about(keys[9], (SHORT - 1, 3, D), 1.0, 6.0, ((2, 4),), jnp.float32)
    conv_history = scatter_about(keys[10], (HISTORY, D), 1.0, 6.0, ((1, 4),), jnp.float32)
    long_filter = draw_long_filter(jax.random.fold_in(keys[13], 71), 0)
    hyena_out_weight = scatter_about(keys[12], (D, D), D ** -0.5, 0.09375, ((0, 4), (1, 32)))
    return {"span_input": span_input, "norm_gain": norm_gain, "query_key_value_weight": query_key_value_weight, "cache_keys": cache_keys, "cache_values": cache_values, "attn_out_weight": attn_out_weight, "mixer_gain": mixer_gain, "hyena_in_weight": hyena_in_weight, "short_filter": short_filter, "short_history": short_history, "conv_history": conv_history, "long_filter": long_filter, "hyena_out_weight": hyena_out_weight}


EPSILON = 1e-06

def inverse_rms(values):
    return lax.rsqrt(lax.optimization_barrier(jnp.mean(values * values, axis=1, keepdims=True)) + EPSILON)

def head_partial(queries, key_block, value_block, own_keys, own_values, visible, head_id):
    offset = head_id * HDIM
    softmax_scale = HDIM ** (-0.5)
    query_head = lax.dynamic_slice_in_dim(queries, offset, HDIM, 1)
    head_of_keys = lax.dynamic_slice_in_dim(key_block, offset, HDIM, 1)
    value_head = lax.dynamic_slice_in_dim(value_block, offset, HDIM, 1)
    own_key_head = lax.dynamic_slice_in_dim(own_keys, offset, HDIM, 1)
    own_value_head = lax.dynamic_slice_in_dim(own_values, offset, HDIM, 1)
    scores = jnp.dot(query_head, head_of_keys.T, preferred_element_type=jnp.float32) * softmax_scale
    own_scores = jnp.dot(query_head, own_key_head.T, preferred_element_type=jnp.float32) * softmax_scale
    own_scores = jnp.where(visible, own_scores, -jnp.inf)
    top = jnp.maximum(lax.optimization_barrier(jnp.max(scores, axis=1)), lax.optimization_barrier(jnp.max(own_scores, axis=1)))
    probs = jnp.exp(scores - top[:, None])
    own_probs = jnp.exp(own_scores - top[:, None])
    totals = lax.optimization_barrier(jnp.sum(probs, axis=1)) + lax.optimization_barrier(jnp.sum(own_probs, axis=1))
    weighted = jnp.dot(probs.astype(jnp.bfloat16), value_head, preferred_element_type=jnp.float32)
    weighted = weighted + jnp.dot(own_probs.astype(jnp.bfloat16), own_value_head, preferred_element_type=jnp.float32)
    return (top, totals, weighted)

def block_partial(queries, cache_keys, cache_values, new_keys, new_values, block_id):
    key_block = lax.dynamic_slice_in_dim(cache_keys, block_id * CACHE_DEV, CACHE_DEV, 0)
    value_block = lax.dynamic_slice_in_dim(cache_values, block_id * CACHE_DEV, CACHE_DEV, 0)
    own_keys = lax.dynamic_slice_in_dim(new_keys, block_id * TOK_DEV, TOK_DEV, 0)
    own_values = lax.dynamic_slice_in_dim(new_values, block_id * TOK_DEV, TOK_DEV, 0)
    key_places = block_id * TOK_DEV + jnp.arange(TOK_DEV, dtype=jnp.int32)
    visible = key_places[None, :] <= jnp.arange(SPAN, dtype=jnp.int32)[:, None]

    def one_head(head_id):
        return head_partial(queries, key_block, value_block, own_keys, own_values, visible, head_id)
    return lax.map(one_head, jnp.arange(HEADS, dtype=jnp.int32))

def reference(span_input, norm_gain, query_key_value_weight, cache_keys, cache_values, attn_out_weight, mixer_gain, hyena_in_weight, short_filter, short_history, conv_history, long_filter, hyena_out_weight):
    inputs = span_input.astype(jnp.float32)
    normalized_rows = (inputs * inverse_rms(inputs) * norm_gain.astype(jnp.float32)).astype(jnp.bfloat16)
    projected = jnp.dot(normalized_rows, query_key_value_weight.reshape(D, 3 * D), preferred_element_type=jnp.float32)
    projected = projected.reshape(SPAN, 3, D).astype(jnp.bfloat16)
    queries = projected[:, 0]
    new_keys = projected[:, 1]
    new_values = projected[:, 2]

    def one_block(block_id):
        return block_partial(queries, cache_keys, cache_values, new_keys, new_values, block_id)
    tops, totals, weighted = lax.map(one_block, jnp.arange(N_CTX, dtype=jnp.int32))
    top_all = lax.optimization_barrier(jnp.max(tops, axis=0))
    factors = jnp.exp(tops - top_all[None])
    total_all = lax.optimization_barrier(jnp.sum(factors * totals, axis=0))
    acc = lax.optimization_barrier(jnp.sum(factors[..., None] * weighted, axis=0))
    attended = (acc / total_all[..., None]).astype(jnp.bfloat16)
    attended = jnp.transpose(attended, (1, 0, 2)).reshape(SPAN, D)
    hidden = inputs + jnp.dot(attended, attn_out_weight, preferred_element_type=jnp.float32)
    normed_mix = (hidden * inverse_rms(hidden) * mixer_gain.astype(jnp.float32)).astype(jnp.bfloat16)
    features = jnp.dot(normed_mix, hyena_in_weight.reshape(D, 3 * D), preferred_element_type=jnp.float32)
    features = features.reshape(SPAN, 3, D)
    extended = jnp.concatenate([short_history, features], axis=0)
    filtered = jnp.zeros((SPAN, 3, D), jnp.float32)
    for lag_index in range(SHORT):
        begin = SHORT - 1 - lag_index
        filtered = filtered + short_filter[lag_index][None] * extended[begin:begin + SPAN]
    product = filtered[:, 1] * filtered[:, 2]
    padded_product = jnp.concatenate([conv_history, product], axis=0)
    convolved = jnp.zeros((SPAN, D), jnp.float32)
    for lag_index in range(FILT):
        begin = HISTORY - lag_index
        convolved = convolved + long_filter[lag_index][None] * padded_product[begin:begin + SPAN]
    gated = (filtered[:, 0] * convolved).astype(jnp.bfloat16)
    mixed = hidden + jnp.dot(gated, hyena_out_weight, preferred_element_type=jnp.float32)
    return mixed.astype(jnp.bfloat16)
```

```python
import functools
import math

import jax
import jax.numpy as jnp
from jax import lax
from jax.experimental import pallas as pl
from jax.experimental.pallas import tpu as pltpu
from jax.sharding import PartitionSpec as P

D = 4096
HDIM = 128
EPSILON = 1e-06
EXP_SCALE = HDIM ** (-0.5) * math.log2(math.e)
VMEM_LIMIT = 48 * 1024 * 1024
STAT_ROWS = 16
STAT_LANES = 128


def params():
    return pltpu.CompilerParams(vmem_limit_bytes=VMEM_LIMIT)


def thirds(value):
    high = value.astype(jnp.bfloat16).astype(jnp.float32)
    rest = value - high
    middle = rest.astype(jnp.bfloat16).astype(jnp.float32)
    return high, middle, rest - middle


def exchange(rows):
    return lax.all_to_all(rows, "ctx", 0, 0, tiled=True)


def project_kernel(x_ref, gain_ref, weight_ref, out_ref):
    x = x_ref[...].astype(jnp.float32)
    squares = jnp.sum(x * x, axis=1, keepdims=True)
    scaled = (x * gain_ref[...].astype(jnp.float32)).astype(jnp.bfloat16)
    width = weight_ref.shape[2]
    for part in range(3):
        term = jnp.dot(scaled, weight_ref[part], preferred_element_type=jnp.float32)
        out_ref[:, part * width : (part + 1) * width] = term.astype(jnp.bfloat16)
    lane = lax.broadcasted_iota(jnp.int32, (x.shape[0], STAT_LANES), 1)
    high, middle, low = thirds(squares)
    stats = jnp.where(lane == 0, high, jnp.where(lane == 1, middle, jnp.where(lane == 2, low, 0.0)))
    out_ref[:, 3 * width :] = stats.astype(jnp.bfloat16)


def project(x, gain, weight):
    rows, width = x.shape[0], weight.shape[2]
    return pl.pallas_call(
        project_kernel,
        out_shape=jax.ShapeDtypeStruct((rows, 3 * width + STAT_LANES), jnp.bfloat16),
        compiler_params=params(),
    )(x, gain, weight)


def reduce_kernel(count, terms_ref, query_ref, key_ref, value_ref):
    tokens = terms_ref.shape[0] // count
    width = query_ref.shape[1]

    def total(begin, size):
        block = terms_ref[:, begin : begin + size].astype(jnp.float32)
        return jnp.sum(block.reshape(count, tokens, size), axis=0)

    stats = total(3 * width, STAT_LANES)
    squares = jnp.sum(stats, axis=1, keepdims=True)
    inv = lax.rsqrt(squares / D + EPSILON)
    for begin in range(0, width, HDIM):
        lanes = slice(begin, begin + HDIM)
        query = (total(begin, HDIM) * inv).astype(jnp.bfloat16)
        query_ref[:, lanes] = jnp.concatenate([query] * count, axis=0)
        pad = jnp.zeros((tokens, HDIM), jnp.float32)
        key = jnp.concatenate([total(width + begin, HDIM) * inv, pad], axis=0)
        key_ref[:, lanes] = key.astype(jnp.bfloat16)
        value = jnp.concatenate([total(2 * width + begin, HDIM) * inv, pad], axis=0)
        value_ref[:, lanes] = value.astype(jnp.bfloat16)


def reduce_projection(terms, count, width):
    rows = terms.shape[0]
    tokens = rows // count
    return pl.pallas_call(
        functools.partial(reduce_kernel, count),
        out_shape=(
            jax.ShapeDtypeStruct((rows, width), jnp.bfloat16),
            jax.ShapeDtypeStruct((2 * tokens, width), jnp.bfloat16),
            jax.ShapeDtypeStruct((2 * tokens, width), jnp.bfloat16),
        ),
        compiler_params=params(),
    )(terms)


def attend_kernel(
    tokens, first_ref, query_ref, key_ref, value_ref, own_key_ref, own_value_ref, out_ref, scores_ref
):
    head = pl.program_id(0)
    heads = pl.num_programs(0)
    contract_last = (((1,), (1,)), ((), ()))
    rows = query_ref.shape[0]
    keys = key_ref.shape[0]
    chunk = 512
    query = query_ref[...]
    own = lax.dot_general(
        query, own_key_ref[...], contract_last, preferred_element_type=jnp.float32
    )
    place = lax.broadcasted_iota(jnp.int32, own.shape, 1)
    row = lax.broadcasted_iota(jnp.int32, own.shape, 0)
    seen = (place < tokens) & (place + first_ref[0] <= row)
    own = jnp.where(seen, own, -jnp.inf)
    running = jnp.full((rows, HDIM), -jnp.inf, jnp.float32)
    for begin in range(0, keys, chunk):
        part = lax.dot_general(
            query, key_ref[begin : begin + chunk, :], contract_last, preferred_element_type=jnp.float32
        )
        scores_ref[:, begin : begin + chunk] = part
        for lane in range(0, chunk, HDIM):
            running = jnp.maximum(running, part[:, lane : lane + HDIM])
    top = jnp.maximum(
        jnp.max(running, axis=1, keepdims=True), jnp.max(own, axis=1, keepdims=True)
    )
    own_probs = jnp.exp2((own - top) * EXP_SCALE)
    acc = jnp.dot(
        own_probs.astype(jnp.bfloat16), own_value_ref[...], preferred_element_type=jnp.float32
    )
    summed = jnp.zeros((rows, HDIM), jnp.float32)
    for begin in range(0, keys, chunk):
        probs = jnp.exp2((scores_ref[:, begin : begin + chunk] - top) * EXP_SCALE)
        for lane in range(0, chunk, HDIM):
            summed = summed + probs[:, lane : lane + HDIM]
        acc = acc + jnp.dot(
            probs.astype(jnp.bfloat16),
            value_ref[begin : begin + chunk, :],
            preferred_element_type=jnp.float32,
        )
    total = jnp.sum(summed, axis=1, keepdims=True) + jnp.sum(own_probs, axis=1, keepdims=True)
    out_ref[:, pl.ds(pl.multiple_of(head * HDIM, HDIM), HDIM)] = acc.astype(jnp.bfloat16)
    width = out_ref.shape[1] - STAT_LANES
    stat_lane = lax.broadcasted_iota(jnp.int32, (rows, STAT_LANES), 1) - head * 6
    stats = out_ref[:, width:].astype(jnp.float32)
    stats = jnp.where(head == 0, 0.0, stats)
    for index, part in enumerate(thirds(top) + thirds(total)):
        stats = jnp.where(stat_lane == index, part, stats)
    out_ref[:, width:] = stats.astype(jnp.bfloat16)


def attend(first, queries, keys, values, own_keys, own_values, tokens):
    rows, width = queries.shape
    heads = width // HDIM
    context = keys.shape[0]
    own_rows = own_keys.shape[0]
    return pl.pallas_call(
        functools.partial(attend_kernel, tokens),
        grid=(heads,),
        in_specs=[
            pl.BlockSpec(memory_space=pltpu.SMEM),
            pl.BlockSpec((rows, HDIM), lambda h: (0, h)),
            pl.BlockSpec((context, HDIM), lambda h: (0, h)),
            pl.BlockSpec((context, HDIM), lambda h: (0, h)),
            pl.BlockSpec((own_rows, HDIM), lambda h: (0, h)),
            pl.BlockSpec((own_rows, HDIM), lambda h: (0, h)),
        ],
        out_specs=pl.BlockSpec((rows, width + STAT_LANES), lambda h: (0, 0)),
        out_shape=jax.ShapeDtypeStruct((rows, width + STAT_LANES), jnp.bfloat16),
        scratch_shapes=[pltpu.VMEM((rows, context), jnp.float32)],
        compiler_params=params(),
        cost_estimate=pl.CostEstimate(
            flops=4 * rows * context * width,
            bytes_accessed=4 * context * width,
            transcendentals=rows * context * heads,
        ),
    )(first, queries, keys, values, own_keys, own_values)


def combine_kernel(count, parts_ref, out_ref):
    rows, width = out_ref.shape
    tokens = rows // count
    stats = parts_ref[:, width:].astype(jnp.float32).reshape(count, tokens, STAT_LANES)
    for head in range(width // HDIM):
        lanes = slice(head * HDIM, (head + 1) * HDIM)
        base = head * 6
        tops = stats[:, :, base : base + 1] + stats[:, :, base + 1 : base + 2]
        tops = tops + stats[:, :, base + 2 : base + 3]
        totals = stats[:, :, base + 3 : base + 4] + stats[:, :, base + 4 : base + 5]
        totals = totals + stats[:, :, base + 5 : base + 6]
        top = jnp.max(tops, axis=0, keepdims=True)
        factors = jnp.exp2((tops - top) * EXP_SCALE)
        total = jnp.sum(factors * totals, axis=0)
        acc = parts_ref[:, lanes].astype(jnp.float32).reshape(count, tokens, HDIM)
        acc = jnp.sum(factors * acc, axis=0)
        attended = (acc / total).astype(jnp.bfloat16)
        out_ref[:, lanes] = jnp.concatenate([attended] * count, axis=0)


def combine(parts, count):
    rows, width = parts.shape
    return pl.pallas_call(
        functools.partial(combine_kernel, count),
        out_shape=jax.ShapeDtypeStruct((rows, width - STAT_LANES), jnp.bfloat16),
        compiler_params=params(),
    )(parts)


def feature_kernel(count, terms_ref, x_ref, gain_ref, weight_ref, hidden_ref, out_ref):
    hidden = x_ref[...].astype(jnp.float32)
    for term in range(terms_ref.shape[0]):
        hidden = hidden + terms_ref[term]
    hidden_ref[...] = hidden
    turned = hidden.T
    scaled = (hidden * gain_ref[...].astype(jnp.float32)).T.astype(jnp.bfloat16)
    squares = jnp.sum(turned * turned, axis=0, keepdims=True)
    columns = weight_ref.shape[2]
    per_device = columns // count
    message = 3 * per_device + STAT_ROWS
    row = lax.broadcasted_iota(jnp.int32, (STAT_ROWS, hidden.shape[0]), 0)
    high, middle, low = thirds(squares)
    stats = jnp.where(row == 0, high, jnp.where(row == 1, middle, jnp.where(row == 2, low, 0.0)))
    stats = stats.astype(jnp.bfloat16)
    chunk = 256
    for part in range(3):
        for begin in range(0, columns, chunk):
            term = lax.dot_general(
                weight_ref[part, :, begin : begin + chunk],
                scaled,
                (((0,), (0,)), ((), ())),
                preferred_element_type=jnp.float32,
            ).astype(jnp.bfloat16)
            for piece in range(chunk // per_device):
                place = (begin // per_device + piece) * message + part * per_device
                out_ref[place : place + per_device, :] = term[
                    piece * per_device : (piece + 1) * per_device
                ]
    for device in range(count):
        place = device * message + 3 * per_device
        out_ref[place : place + STAT_ROWS, :] = stats


def feature_terms(terms, x, gain, weight, count):
    rows, width = x.shape
    columns = weight.shape[2]
    message = 3 * (columns // count) + STAT_ROWS
    return pl.pallas_call(
        functools.partial(feature_kernel, count),
        out_shape=(
            jax.ShapeDtypeStruct((rows, width), jnp.float32),
            jax.ShapeDtypeStruct((count * message, rows), jnp.bfloat16),
        ),
        compiler_params=params(),
    )(terms, x, gain, weight)


def mix_kernel(count, terms_ref, tables_ref, out_ref):
    per_device = tables_ref.shape[0]
    message = terms_ref.shape[0] // count
    rows = terms_ref.shape[1]
    summed = jnp.zeros((message, rows), jnp.float32)
    for device in range(count):
        summed = summed + terms_ref[device * message : (device + 1) * message, :].astype(jnp.float32)
    squares = summed[3 * per_device : 3 * per_device + 1]
    squares = squares + summed[3 * per_device + 1 : 3 * per_device + 2]
    squares = squares + summed[3 * per_device + 2 : 3 * per_device + 3]
    inv = lax.rsqrt(squares / D + EPSILON)
    history = tables_ref[:, :HDIM]
    taps = tables_ref[:, HDIM : 2 * HDIM]
    small = tables_ref[:, 2 * HDIM :]
    lane = lax.broadcasted_iota(jnp.int32, (per_device, HDIM), 1)
    filtered = []
    for part in range(3):
        features = summed[part * per_device : (part + 1) * per_device] * inv
        older = small[:, 9 + part : 10 + part]
        newer = small[:, 12 + part : 13 + part]
        before = jnp.where(lane == HDIM - 2, older, jnp.where(lane == HDIM - 1, newer, 0.0))
        extended = jnp.concatenate([before, features], axis=1)
        result = small[:, part : part + 1] * features
        for lag in range(1, 3):
            column = lag * 3 + part
            moved = pltpu.roll(extended, lag, 1)[:, HDIM:]
            result = result + small[:, column : column + 1] * moved
        filtered.append(result)
    extended = jnp.concatenate([history, filtered[1] * filtered[2]], axis=1)
    convolved = taps[:, 0:1] * extended[:, HDIM:]
    for lag in range(1, HDIM):
        moved = pltpu.roll(extended, lag, 1)[:, HDIM:]
        convolved = convolved + taps[:, lag : lag + 1] * moved
    gated = (filtered[0] * convolved).astype(jnp.bfloat16)
    for device in range(count):
        out_ref[device * per_device : (device + 1) * per_device, :] = gated


def mix(terms, tables, count):
    per_device = tables.shape[0]
    return pl.pallas_call(
        functools.partial(mix_kernel, count),
        out_shape=jax.ShapeDtypeStruct((count * per_device, terms.shape[1]), jnp.bfloat16),
        compiler_params=params(),
    )(terms, tables)


def own_tables(rank, per_device, short_filter, short_history, conv_history, long_filter):
    begin = rank * per_device

    def own(value):
        flat = value.reshape((-1, value.shape[-1]))
        return lax.dynamic_slice_in_dim(flat, begin, per_device, 1)

    pieces = [own(conv_history), own(long_filter), own(short_filter), own(short_history)]
    used = sum(piece.shape[0] for piece in pieces) + 1
    first = jnp.zeros((1, per_device), jnp.float32)
    last = jnp.zeros((3 * HDIM - used, per_device), jnp.float32)
    return jnp.concatenate([first] + pieces + [last], axis=0).T


def shards(
    span_input,
    norm_gain,
    query_key_value_weight,
    cache_keys,
    cache_values,
    attn_out_weight,
    mixer_gain,
    hyena_in_weight,
    short_filter,
    short_history,
    conv_history,
    long_filter,
    hyena_out_weight,
):
    rank = lax.axis_index("ctx")
    count = lax.axis_size("ctx")
    rows = span_input.shape[0]
    tokens = rows // count
    width = query_key_value_weight.shape[2]
    per_device = hyena_in_weight.shape[2] // count

    terms = project(
        span_input, norm_gain[None, :], jnp.transpose(query_key_value_weight, (1, 0, 2))
    )
    queries, own_keys, own_values = reduce_projection(exchange(terms), count, width)
    queries = exchange(queries)
    first = jnp.reshape(rank * tokens, (1,)).astype(jnp.int32)
    parts = attend(first, queries, cache_keys, cache_values, own_keys, own_values, tokens)
    attended = exchange(combine(exchange(parts), count))
    attn_term = jnp.dot(attended, attn_out_weight, preferred_element_type=jnp.float32)
    attn_terms = lax.all_gather(attn_term, "tp")
    hidden, feature_sends = feature_terms(
        attn_terms,
        span_input,
        mixer_gain[None, :],
        jnp.transpose(hyena_in_weight, (1, 0, 2)),
        count,
    )
    tables = own_tables(
        rank, per_device, short_filter, short_history, conv_history, long_filter
    )
    gated = exchange(mix(exchange(feature_sends), tables, count))
    mixer_term = lax.dot_general(
        gated, hyena_out_weight, (((0,), (0,)), ((), ())), preferred_element_type=jnp.float32
    )
    mixer = jnp.sum(lax.all_gather(mixer_term, "tp"), axis=0)
    return (hidden + mixer).astype(jnp.bfloat16)


def solution(mesh):
    return jax.shard_map(
        shards,
        mesh=mesh,
        in_specs=(
            P(None, "ctx"),
            P("ctx"),
            P("ctx", None, "tp"),
            P("ctx", "tp"),
            P("ctx", "tp"),
            P("tp", "ctx"),
            P("ctx"),
            P("ctx", None, "tp"),
            P(None, None, "tp"),
            P(None, None, "tp"),
            P(None, "tp"),
            P(None, "tp"),
            P("tp", "ctx"),
        ),
        out_specs=P(None, "ctx"),
        check_vma=False,
    )
```
